32 devices in a mesh: parts: 2 (over x), tile: 16 (over z, y, core).
Axes of the slice: x: 2, y: 2, z: 4, core: 2. Of those that a mesh axis runs over, the one named last changes fastest.
Arguments:
- planes: bfloat16 [3, 256, 2048], P(None, ('parts', 'tile')), parts along dimension 1, may hold values from -9 to 9
- decoder_in: float32 [32, 64], replicated, may hold values from -1 to 1
- decoder_out: float32 [64, 4], replicated, may hold values from -3 to 3
- corner: int32 [3, 2097152], P(None, ('parts', 'tile')), parts along dimension 1, may hold values from 0 to 48
- fraction: float32 [3, 2, 2097152], P(None, None, ('parts', 'tile')), parts along dimension 2, may hold values from 0 to 1
- block_slot: int32 [3, 16384], P(None, ('parts', 'tile')), parts along dimension 1, may hold values from 0 to 15, as said below
- wanted: int32 [32, 3, 16, 1], P(('parts', 'tile')), parts along dimension 0, may hold values from 0 to 7, as said below
- ray_id: int32 [32, 65536], P(('parts', 'tile')), parts along dimension 0, may hold values from 0 to 255, never falling along the last dimension, each value on 1 to 512 neighbouring positions
- ray_grad: float32 [32, 4, 256], P(('parts', 'tile')), parts along dimension 0, may hold values from -6 to 6
Outputs:
- plane_grad: float32 [3, 256, 2048], P(None, ('parts', 'tile')), parts along dimension 1
The draws below stay inside these ranges and needn't reach their ends.
There are 2 independent parts, one for each index of `parts`. The reference program is written for one: setup_inputs(seed, part) draws one part's arguments, and reference() takes and returns one part's arrays. A program takes and returns all parts, laid end to end along the dimension named above; an argument that names none is the same for every part. Nothing has to cross between parts.
Inputs may be any that keep to these rules, and one draw needn't show every extreme that they name: `wanted`: for each requesting device, plane and owner, the 1 entries are distinct. `block_slot`: the 512 blocks of one device name every one of its 16 list entries at least once, for each plane.
All inputs are finite; a program needn't handle non-finite values.
Results may differ from the reference program's by a relative error of at most 0.0062.
Values may be sent and summed in bfloat16 or wider, within the bound.
A program may use at most 64 MiB of HBM per device.

```python
import math
import jax
import jax.numpy as jnp
import numpy as np
from jax import lax

C = 32
HID = 64
OUTS = 4
TS = 8
BLK = 128
CAP = 1
TILES_DEV = 8
BLOCKS_DEV = 512
RAYS_DEV = 256
OWNERS = 16
CELLS = 64
FEAT = 2048
SLOTS = 16
TILES = 128
BLOCKS = 8192
SAMP_DEV = 65536
SAMPLES = 1048576
RAY_MOST = 512


def draw_wanted(key, part):
    key = jax.random.fold_in(key, 11)
    first_key, second_key = jax.random.split(key)
    favour = jax.random.randint(first_key, (1, 1, OWNERS, TILES_DEV), 0, 1 << 20)
    noise = jax.random.randint(second_key, (OWNERS, 3, OWNERS, TILES_DEV), 0, 1 << 20)
    order = jnp.arange(TILES_DEV, dtype=jnp.int32)
    scores = (noise + favour) * TILES_DEV + order
    ranked = jnp.argsort(scores, axis=-1)
    return ranked[..., :CAP].astype(jnp.int32)


def draw_block_slot(key, part):
    key = jax.random.fold_in(key, 23)

    def one_device(device_key):
        base_key, extra_key, mix_key = jax.random.split(device_key, 3)
        base = jax.random.permutation(base_key, SLOTS).astype(jnp.int32)
        extra = jax.random.randint(extra_key, (BLOCKS_DEV - SLOTS,), 0, SLOTS).astype(jnp.int32)
        joined = jnp.concatenate([base, extra])
        return jax.random.permutation(mix_key, joined).astype(jnp.int32)
    device_keys = jax.random.split(key, 3 * OWNERS)
    slots_all = jax.vmap(one_device)(device_keys)
    return slots_all.reshape(3, BLOCKS).astype(jnp.int32)


def with_ends(array, key, least, largest):
    shape = array.shape
    place = [jax.random.randint(jax.random.fold_in(key, axis), (), 0, shape[axis]) for axis in range(len(shape))]
    array = array.at[tuple(place)].set(least)
    longest = shape.index(max(shape))
    place[longest] = (place[longest] + 1) % shape[longest]
    return array.at[tuple(place)].set(largest)


def level_of(key, dims, cuts, least, top_value):
    level, own = 1.0, jax.random.fold_in(key, 6)
    for axis_at, blocks in cuts:
        steps = jnp.exp(jax.random.uniform(jax.random.fold_in(own, axis_at), (blocks,), jnp.float32, least / len(cuts), top_value / len(cuts)))
        level = level * jnp.repeat(steps, dims[axis_at] // blocks).reshape([-1 if axis == axis_at else 1 for axis in range(len(dims))])
    return level


def length_profile(number_of, total, reach, skew):
    loads = [(1 << 20) // math.isqrt(standing ** skew) + 1 for standing in range(2, number_of + 1)]
    rest, holding = total - reach - (number_of - 1), [1] * (number_of - 1)
    while rest > 0:
        candidates = [i for i in range(number_of - 1) if holding[i] < reach]
        pool, left = sum([loads[i] for i in candidates]), rest
        for i in candidates:
            more = min(reach - holding[i], max(1, left * loads[i] // pool), rest)
            holding[i] = holding[i] + more
            rest = rest - more
    return np.array([reach] + holding)


def ragged(key, number_of, total, limit, slope):
    if number_of == 2:
        one = jax.random.randint(key, (), max(1, total - limit), min(limit, total - 1) + 1)
        return jnp.stack([one, total - one])
    sizes = jnp.asarray(length_profile(number_of, total, limit, slope), jnp.int32)
    twos = (number_of - 1) // 2
    source_of, taker = sizes[1:1 + 2 * twos:2], sizes[2:2 + 2 * twos:2]
    room = jnp.minimum(source_of - 1, limit - taker)
    passed = jax.random.randint(jax.random.fold_in(key, 1), (twos,), 0, 1 << 20) % (room + 1)
    sizes = sizes.at[1:1 + 2 * twos:2].set(source_of - passed).at[2:2 + 2 * twos:2].set(taker + passed)
    return sizes[jax.random.permutation(jax.random.fold_in(key, 2), number_of)]


def scatter_about(rng, extent, scale, limit, shards=(), kind=jnp.bfloat16):
    result = jax.random.normal(rng, extent, jnp.float32) * scale
    if len(shards) > 0:
        result = level_of(rng, extent, shards, -0.22, 0.18) * result
    return jnp.clip(result, min=-limit, max=limit).astype(kind)


def setup_inputs(seed: int = 0, part: int = 0) -> dict:
    key_of = jax.random.split(jax.random.key(seed), 10)
    part_keys = jax.random.split(jax.random.fold_in(key_of[9], part), 10)
    planes = scatter_about(part_keys[0], (3, TILES, FEAT), 1.5, 9.0, ((1, 16),))
    decoder_in = scatter_about(key_of[1], (C, HID), C ** -0.5, 1.0, (), jnp.float32)
    decoder_out = scatter_about(key_of[2], (HID, OUTS), OUTS ** -0.5, 3.0, (), jnp.float32)
    corner = with_ends(jax.random.randint(part_keys[3], (3, SAMPLES), 0, (TS - 1) * (TS - 1)), jax.random.fold_in(part_keys[3], 1), 0, ((TS - 1) * (TS - 1)) - 1).astype(jnp.int32)
    fraction = jnp.clip(1.0 * jax.random.uniform(part_keys[4], (3, 2, SAMPLES), jnp.float32) ** level_of(part_keys[4], (3, 2, SAMPLES), ((2, 16),), -0.2, 0.2), 0.0, 1.0)
    block_slot = draw_block_slot(jax.random.fold_in(jax.random.fold_in(key_of[9], part), 71), part)
    wanted = draw_wanted(jax.random.fold_in(jax.random.fold_in(key_of[9], part), 71), part)
    ray_id = jax.vmap(lambda own: jnp.searchsorted(jnp.cumsum(ragged(own, RAYS_DEV, SAMP_DEV, RAY_MOST, 1)), jnp.arange(SAMP_DEV), side="right"))(jax.random.split(part_keys[7], OWNERS)).reshape((OWNERS, SAMP_DEV)).astype(jnp.int32)
    ray_grad = scatter_about(part_keys[8], (OWNERS, OUTS, RAYS_DEV), 1.0, 6.0, ((0, 16),), jnp.float32)
    return dict(planes=planes, decoder_in=decoder_in, decoder_out=decoder_out, corner=corner, fraction=fraction, block_slot=block_slot, wanted=wanted, ray_id=ray_id, ray_grad=ray_grad)


def corner_weights(corner_row, fraction_row):
    corner_cell = (corner_row // (TS - 1)) * TS + corner_row % (TS - 1)
    cell_ids = jnp.stack([corner_cell, corner_cell + 1, corner_cell + TS, corner_cell + TS + 1]).astype(jnp.int32)
    across = fraction_row[0]
    downward = fraction_row[1]
    weights = jnp.stack([(1.0 - across) * (1.0 - downward), across * (1.0 - downward), (1.0 - across) * downward, across * downward])
    weights = lax.optimization_barrier(weights.astype(jnp.bfloat16)).astype(jnp.float32)
    return cell_ids, weights


def reference(planes, decoder_in, decoder_out, corner, fraction, block_slot, wanted, ray_id, ray_grad):
    tables = planes.reshape(3, TILES, C, CELLS)
    corner_dev = corner.reshape(3, OWNERS, SAMP_DEV).transpose(1, 0, 2)
    fraction_dev = fraction.reshape(3, 2, OWNERS, SAMP_DEV).transpose(2, 0, 1, 3)
    slot_dev = block_slot.reshape(3, OWNERS, BLOCKS_DEV).transpose(1, 0, 2)

    def device_step(totals, inputs):
        corner_d, fraction_d, slot_d, wanted_d, rays_d, grad_d = inputs
        tile_list, cell_list, weight_list, features = [], [], [], []
        for which in range(3):
            slot_ids = jnp.repeat(slot_d[which], BLK)
            owner_ids = slot_ids // CAP
            tile_ids = (owner_ids * TILES_DEV + wanted_d[which, owner_ids, slot_ids % CAP]).astype(jnp.int32)
            cell_ids, weights = corner_weights(corner_d[which], fraction_d[which])
            feature = jnp.zeros((SAMP_DEV, C), jnp.float32)
            for corner_idx in range(4):
                values = tables[which][tile_ids, :, cell_ids[corner_idx]].astype(jnp.float32)
                feature = feature + weights[corner_idx][:, None] * values
            tile_list.append(tile_ids)
            cell_list.append(cell_ids)
            weight_list.append(weights)
            features.append(feature)
        product = features[0] * features[1] * features[2]
        pre = jnp.dot(product, decoder_in, precision=lax.Precision.HIGHEST)
        out_grad = grad_d[:, rays_d].T
        hidden_grad = jnp.dot(out_grad, decoder_out.T, precision=lax.Precision.HIGHEST)
        sigmoid_pre = jax.nn.sigmoid(pre)
        pre_grad = hidden_grad * sigmoid_pre * (1.0 + pre * (1.0 - sigmoid_pre))
        prod_grad = jnp.dot(pre_grad, decoder_in.T, precision=lax.Precision.HIGHEST)
        new_totals = []
        for which in range(3):
            others = features[(which + 1) % 3] * features[(which + 2) % 3]
            feat_grad = lax.optimization_barrier((prod_grad * others).astype(jnp.bfloat16)).astype(jnp.float32)
            total = totals[which]
            for corner_idx in range(4):
                total = total.at[tile_list[which], :, cell_list[which][corner_idx]].add(weight_list[which][corner_idx][:, None] * feat_grad)
            new_totals.append(total)
        return tuple(new_totals), None

    start = tuple(jnp.zeros((TILES, C, CELLS), jnp.float32) for which in range(3))
    totals, unused = lax.scan(device_step, start, (corner_dev, fraction_dev, slot_dev, wanted, ray_id, ray_grad))
    return jnp.stack(totals).reshape(3, TILES, FEAT)
```

```python
import functools

import jax
import jax.numpy as jnp
from jax import lax
from jax.experimental import pallas as pl
from jax.experimental.pallas import tpu as pltpu
from jax.sharding import PartitionSpec as P

OUTS = 4
TS = 8
BLK = 128
CHUNK = 8192
GROUP = 16
UNROLL = 1

F32 = jnp.float32
BF16 = jnp.bfloat16


def cell_weights(corner_row, across, downward):
    row = (corner_row * 37) >> 8
    col = corner_row - row * (TS - 1)
    sub = lax.broadcasted_iota(jnp.int32, (TS, BLK), 0)
    col8 = jnp.broadcast_to(col, (TS, BLK))
    side = jnp.where(sub == col8, 1.0 - across, jnp.where(sub == col8 + 1, across, 0.0))
    upper = side * (1.0 - downward)
    lower = side * downward
    upper = jnp.concatenate([upper, upper], axis=0).astype(BF16)
    lower = jnp.concatenate([lower, lower], axis=0).astype(BF16)
    row8 = jnp.broadcast_to(row, (TS, BLK)).astype(F32)
    rows = jnp.concatenate([row8, row8 - 1.0], axis=0).astype(BF16)
    zero = jnp.zeros((2 * TS, BLK), BF16)
    pairs = []
    for first in range(0, TS, 2):
        here = rows == jnp.asarray(first, BF16)
        above = rows == jnp.asarray(first - 1, BF16)
        pairs.append(jnp.where(here, upper, jnp.where(above, lower, zero)))
    return jnp.concatenate(pairs, axis=0)


def dot(a, b):
    return jnp.dot(a, b, preferred_element_type=F32)


def dot_t(a, b):
    return lax.dot_general(a, b, (((1,), (1,)), ((), ())), preferred_element_type=F32)


def compute_kernel(
    slots_ref, tiles_ref, win_t_ref, win_ref, wout_ref, table_ref, corner_ref, fraction_ref, ray_ref, acc_ref
):
    step = pl.program_id(0)

    @pl.when(step == 0)
    def _():
        acc_ref[...] = jnp.zeros_like(acc_ref)

    halves = table_ref.shape[0]
    blocks = CHUNK // BLK

    @functools.partial(lax.fori_loop, 0, blocks // GROUP, init_val=None, unroll=UNROLL)
    def _(at, carry):
        wide, feats, slots = [], [], []
        grads_out = []
        for b in range(GROUP):
            local = at * GROUP + b
            lanes = pl.ds(pl.multiple_of(local * BLK, BLK), BLK)
            wides, fs, ss = [], [], []
            for p in range(3):
                slot = slots_ref[p, step * blocks + local]
                m = cell_weights(
                    corner_ref[p : p + 1, lanes], fraction_ref[p, 0:1, lanes], fraction_ref[p, 1:2, lanes]
                )
                z = jnp.zeros_like(m)
                w = jnp.concatenate(
                    [jnp.concatenate([m, z], axis=1), jnp.concatenate([z, m], axis=1)], axis=0
                )
                f = dot(tiles_ref[p, slot], w)
                fs.append(jnp.concatenate([f[:, :BLK], f[:, BLK:]], axis=0))
                wides.append(w)
                ss.append(slot)
            wide.append(wides)
            feats.append(fs)
            slots.append(ss)
            ray = ray_ref[0:1, lanes]
            rows = table_ref.shape[1]
            picks = []
            idx = jnp.broadcast_to(ray & (BLK - 1), (rows, BLK))
            half = jnp.broadcast_to(ray >> 7, (rows, BLK))
            sub = lax.broadcasted_iota(jnp.int32, (rows, BLK), 0) // OUTS
            for h in range(halves):
                got = jnp.take_along_axis(table_ref[h], idx, axis=1)
                picks.append(jnp.where(half == sub + 2 * h, got, 0.0))
            grads_out.append(jnp.concatenate(picks, axis=0))
        f = [jnp.concatenate([feats[b][p] for b in range(GROUP)], axis=1) for p in range(3)]
        others = [f[1] * f[2], f[0] * f[2], f[0] * f[1]]
        product = (others[2] * f[2]).astype(BF16)
        grads_out = jnp.concatenate(grads_out, axis=1).astype(BF16)
        half_pre = dot(win_t_ref[...], product)
        hidden = dot(wout_ref[...], grads_out)
        t = jnp.tanh(half_pre)
        pre_grad = hidden * ((1.0 + t) * (1.0 + half_pre * (1.0 - t)))
        prod_grad = dot(win_ref[...], pre_grad.astype(BF16))
        for p in range(3):
            fg = (prod_grad * others[p]).astype(BF16)
            half_c = fg.shape[0] // 2
            for b in range(GROUP):
                part = fg[:, b * BLK : (b + 1) * BLK]
                lhs = jnp.concatenate([part[:half_c], part[half_c:]], axis=1)
                slot = slots[b][p]
                acc_ref[p, slot] += dot_t(lhs, wide[b][p])
        return carry


def compute(slots, tiles, decoder_in, decoder_out, ray_table, corner, fraction, ray_id):
    channels, hid = decoder_in.shape
    slot_count = tiles.shape[1]
    samples = corner.shape[1]
    rays = ray_table.shape[1]
    by_parity = jnp.concatenate([decoder_in[0::2], decoder_in[1::2]], axis=0)
    win_t = (by_parity.T * 0.5).astype(BF16)
    win = by_parity.astype(BF16)
    halves = rays // (2 * BLK)
    wout = jnp.concatenate([decoder_out * 0.5] * (2 * halves), axis=1).astype(BF16)
    table = ray_table.reshape(OUTS, halves, 2, BLK).transpose(1, 2, 0, 3).reshape(halves, 2 * OUTS, BLK)
    steps = samples // CHUNK
    vmem = pl.BlockSpec(memory_space=pltpu.VMEM)
    grid_spec = pltpu.PrefetchScalarGridSpec(
        num_scalar_prefetch=1,
        grid=(steps,),
        in_specs=[
            vmem,
            vmem,
            vmem,
            vmem,
            vmem,
            pl.BlockSpec((3, CHUNK), lambda i, s: (0, i)),
            pl.BlockSpec((3, 2, CHUNK), lambda i, s: (0, 0, i)),
            pl.BlockSpec((1, CHUNK), lambda i, s: (0, i)),
        ],
        out_specs=pl.BlockSpec(tiles.shape, lambda i, s: (0, 0, 0, 0)),
    )
    return pl.pallas_call(
        compute_kernel,
        grid_spec=grid_spec,
        out_shape=jax.ShapeDtypeStruct(tiles.shape, F32),
        compiler_params=pltpu.CompilerParams(vmem_limit_bytes=48 * 1024 * 1024),
        name="field_grad",
    )(slots, tiles, win_t, win, wout, table, corner, fraction, ray_id)


def shards(planes, decoder_in, decoder_out, corner, fraction, block_slot, wanted, ray_id, ray_grad):
    owners = lax.axis_size("tile")
    tiles_dev = planes.shape[1]
    row_len = planes.shape[2]
    per_owner = wanted.shape[3]
    slot_count = owners * per_owner
    served = lax.all_to_all(wanted, "tile", split_axis=2, concat_axis=0, tiled=True)
    served = jnp.transpose(served[:, :, 0, :], (1, 0, 2))
    local_ids = jnp.arange(tiles_dev, dtype=jnp.int32)
    serve_pick = (served[..., None] == local_ids).astype(BF16)
    outgoing = jnp.einsum(
        "pock,pkf->pocf", serve_pick, planes, preferred_element_type=F32
    ).astype(BF16)
    incoming = lax.all_to_all(outgoing, "tile", split_axis=1, concat_axis=1, tiled=True)
    tiles = incoming.reshape(3, slot_count, row_len // BLK, BLK)
    slot_sums = compute(block_slot, tiles, decoder_in, decoder_out, ray_grad[0], corner, fraction, ray_id)
    returned = lax.all_to_all(
        slot_sums.reshape(3, owners, per_owner, row_len).astype(BF16),
        "tile",
        split_axis=1,
        concat_axis=1,
        tiled=True,
    )
    returned = returned.reshape(3, slot_count, row_len)
    local_places = jnp.arange(tiles_dev, dtype=jnp.int32)[None, :, None]
    owner_pick = (local_places == served.reshape(3, 1, slot_count)).astype(BF16)
    return jnp.einsum("pts,psf->ptf", owner_pick, returned, preferred_element_type=F32)


def solution(mesh):
    placed = (
        P(None, ("parts", "tile"), None),
        P(),
        P(),
        P(None, ("parts", "tile")),
        P(None, None, ("parts", "tile")),
        P(None, ("parts", "tile")),
        P(("parts", "tile"), None, None, None),
        P(("parts", "tile"), None),
        P(("parts", "tile"), None, None),
    )
    return jax.shard_map(
        shards,
        mesh=mesh,
        in_specs=placed,
        out_specs=P(None, ("parts", "tile"), None),
        check_vma=False,
    )
```

```python
import functools

import jax
import jax.numpy as jnp
from jax import lax
from jax.experimental import pallas as pl
from jax.experimental.pallas import tpu as pltpu
from jax.sharding import PartitionSpec as P

OUTS = 4
TS = 8
BLK = 128
CHUNK = 8192
GROUP = 16
UNROLL = 1

F32 = jnp.float32
BF16 = jnp.bfloat16


def cell_weights(corner_row, across, downward):
    row = (corner_row * 37) >> 8
    col = corner_row - row * (TS - 1)
    sub = lax.broadcasted_iota(jnp.int32, (TS, BLK), 0)
    col8 = jnp.broadcast_to(col, (TS, BLK))
    side = jnp.where(sub == col8, 1.0 - across, jnp.where(sub == col8 + 1, across, 0.0))
    upper = side * (1.0 - downward)
    lower = side * downward
    upper = jnp.concatenate([upper, upper], axis=0).astype(BF16)
    lower = jnp.concatenate([lower, lower], axis=0).astype(BF16)
    row8 = jnp.broadcast_to(row, (TS, BLK)).astype(F32)
    rows = jnp.concatenate([row8, row8 - 1.0], axis=0).astype(BF16)
    zero = jnp.zeros((2 * TS, BLK), BF16)
    pairs = []
    for first in range(0, TS, 2):
        here = rows == jnp.asarray(first, BF16)
        above = rows == jnp.asarray(first - 1, BF16)
        pairs.append(jnp.where(here, upper, jnp.where(above, lower, zero)))
    return jnp.concatenate(pairs, axis=0)


def dot(a, b):
    return jnp.dot(a, b, preferred_element_type=F32)


def dot_t(a, b):
    return lax.dot_general(a, b, (((1,), (1,)), ((), ())), preferred_element_type=F32)


def compute_kernel(
    slots_ref, tiles_ref, win_t_ref, win_ref, wout_ref, table_ref, corner_ref, fraction_ref, ray_ref, acc_ref
):
    step = pl.program_id(0)

    @pl.when(step == 0)
    def _():
        acc_ref[...] = jnp.zeros_like(acc_ref)

    halves = table_ref.shape[0]
    blocks = CHUNK // BLK

    @functools.partial(lax.fori_loop, 0, blocks // GROUP, init_val=None, unroll=UNROLL)
    def _(at, carry):
        wide, feats, slots = [], [], []
        grads_out = []
        for b in range(GROUP):
            local = at * GROUP + b
            lanes = pl.ds(pl.multiple_of(local * BLK, BLK), BLK)
            wides, fs, ss = [], [], []
            for p in range(3):
                slot = slots_ref[p, step * blocks + local]
                m = cell_weights(
                    corner_ref[p : p + 1, lanes], fraction_ref[p, 0:1, lanes], fraction_ref[p, 1:2, lanes]
                )
                z = jnp.zeros_like(m)
                w = jnp.concatenate(
                    [jnp.concatenate([m, z], axis=1), jnp.concatenate([z, m], axis=1)], axis=0
                )
                f = dot(tiles_ref[slot, p], w)
                fs.append(jnp.concatenate([f[:, :BLK], f[:, BLK:]], axis=0))
                wides.append(w)
                ss.append(slot)
            wide.append(wides)
            feats.append(fs)
            slots.append(ss)
            ray = ray_ref[0:1, lanes]
            rows = table_ref.shape[1]
            picks = []
            idx = jnp.broadcast_to(ray & (BLK - 1), (rows, BLK))
            half = jnp.broadcast_to(ray >> 7, (rows, BLK))
            sub = lax.broadcasted_iota(jnp.int32, (rows, BLK), 0) // OUTS
            for h in range(halves):
                got = jnp.take_along_axis(table_ref[h], idx, axis=1)
                picks.append(jnp.where(half == sub + 2 * h, got, 0.0))
            grads_out.append(jnp.concatenate(picks, axis=0))
        f = [jnp.concatenate([feats[b][p] for b in range(GROUP)], axis=1) for p in range(3)]
        others = [f[1] * f[2], f[0] * f[2], f[0] * f[1]]
        product = (others[2] * f[2]).astype(BF16)
        grads_out = jnp.concatenate(grads_out, axis=1).astype(BF16)
        half_pre = dot(win_t_ref[...], product)
        hidden = dot(wout_ref[...], grads_out)
        t = jnp.tanh(half_pre)
        pre_grad = hidden * ((1.0 + t) * (1.0 + half_pre * (1.0 - t)))
        prod_grad = dot(win_ref[...], pre_grad.astype(BF16))
        for p in range(3):
            fg = (prod_grad * others[p]).astype(BF16)
            half_c = fg.shape[0] // 2
            for b in range(GROUP):
                part = fg[:, b * BLK : (b + 1) * BLK]
                lhs = jnp.concatenate([part[:half_c], part[half_c:]], axis=1)
                slot = slots[b][p]
                acc_ref[slot, p] += dot_t(lhs, wide[b][p])
        return carry


def compute(slots, tiles, decoder_in, decoder_out, ray_table, corner, fraction, ray_id):
    channels, hid = decoder_in.shape
    samples = corner.shape[1]
    rays = ray_table.shape[1]
    by_parity = jnp.concatenate([decoder_in[0::2], decoder_in[1::2]], axis=0)
    win_t = (by_parity.T * 0.5).astype(BF16)
    win = by_parity.astype(BF16)
    halves = rays // (2 * BLK)
    wout = jnp.concatenate([decoder_out * 0.5] * (2 * halves), axis=1).astype(BF16)
    table = ray_table.reshape(OUTS, halves, 2, BLK).transpose(1, 2, 0, 3).reshape(halves, 2 * OUTS, BLK)
    steps = samples // CHUNK
    vmem = pl.BlockSpec(memory_space=pltpu.VMEM)
    grid_spec = pltpu.PrefetchScalarGridSpec(
        num_scalar_prefetch=1,
        grid=(steps,),
        in_specs=[
            vmem,
            vmem,
            vmem,
            vmem,
            vmem,
            pl.BlockSpec((3, CHUNK), lambda i, s: (0, i)),
            pl.BlockSpec((3, 2, CHUNK), lambda i, s: (0, 0, i)),
            pl.BlockSpec((1, CHUNK), lambda i, s: (0, i)),
        ],
        out_specs=pl.BlockSpec(tiles.shape, lambda i, s: (0, 0, 0, 0)),
    )
    return pl.pallas_call(
        compute_kernel,
        grid_spec=grid_spec,
        out_shape=jax.ShapeDtypeStruct(tiles.shape, F32),
        compiler_params=pltpu.CompilerParams(vmem_limit_bytes=48 * 1024 * 1024),
        name="field_grad",
    )(slots, tiles, win_t, win, wout, table, corner, fraction, ray_id)


def peer(d, n):
    return {"tile": lax.rem(lax.axis_index("tile") + d, n)}


def enter(n):
    barrier = pltpu.get_barrier_semaphore()

    def tell(d, carry):
        pl.semaphore_signal(barrier, inc=1, device_id=peer(d, n), device_id_type=pl.DeviceIdType.MESH)
        return carry

    lax.fori_loop(1, n, tell, 0)
    pl.semaphore_wait(barrier, n - 1)


def fetch_kernel(
    n, wanted_ref, planes_ref, tiles_ref, asked_ref,
    asking, spread, own, outgoing, ask_send, ask_recv, tile_send, tile_recv,
):
    me = lax.axis_index("tile")
    tiles_dev = planes_ref.shape[1]
    pieces = planes_ref.shape[2] // BLK

    def fill(o, carry):
        for p in range(3):
            asking[o, p : p + 1, :] = jnp.full((1, BLK), wanted_ref[p * n + o], jnp.int32).astype(F32)
        return carry

    asking[...] = jnp.zeros_like(asking)
    lax.fori_loop(0, n, fill, 0)
    enter(n)

    def ask(d):
        to = lax.rem(me + d, n)
        return pltpu.make_async_remote_copy(
            src_ref=asking.at[to], dst_ref=asked_ref.at[me], send_sem=ask_send.at[d], recv_sem=ask_recv.at[d],
            device_id=peer(d, n), device_id_type=pl.DeviceIdType.MESH,
        )

    def asked_by(d):
        source = lax.rem(me - d + n, n)
        return pltpu.make_async_remote_copy(
            src_ref=asking.at[source], dst_ref=asked_ref.at[source], send_sem=ask_send.at[d],
            recv_sem=ask_recv.at[d], device_id=peer(d, n), device_id_type=pl.DeviceIdType.MESH,
        )

    def give(d):
        to = lax.rem(me - d + n, n)
        return pltpu.make_async_remote_copy(
            src_ref=outgoing.at[to], dst_ref=tiles_ref.at[me], send_sem=tile_send.at[d],
            recv_sem=tile_recv.at[d], device_id=peer(n - d, n), device_id_type=pl.DeviceIdType.MESH,
        )

    def given_by(d):
        source = lax.rem(me + d, n)
        return pltpu.make_async_remote_copy(
            src_ref=outgoing.at[source], dst_ref=tiles_ref.at[source], send_sem=tile_send.at[d],
            recv_sem=tile_recv.at[d], device_id=peer(n - d, n), device_id_type=pl.DeviceIdType.MESH,
        )

    def start_ask(d, carry):
        ask(d).start()
        return carry

    lax.fori_loop(1, n, start_ask, 0)
    asked_ref[me] = asking[me]
    for p in range(3):
        wide = planes_ref[p].astype(F32)
        for i in range(pieces):
            spread[p, :, i, :] = wide[:, i * BLK : (i + 1) * BLK]
    own[...] = spread[...].astype(BF16)

    def choose(source, p):
        want = jnp.broadcast_to(asked_ref[source, p : p + 1, :], (pieces, BLK)).astype(BF16)
        got = jnp.zeros((pieces, BLK), BF16)
        for k in range(tiles_dev):
            got = jnp.where(want == jnp.asarray(k, BF16), own[p, k], got)
        return got

    def serve(d, carry):
        asked_by(d).wait_recv()
        to = lax.rem(me - d + n, n)
        for p in range(3):
            outgoing[to, p] = choose(to, p)
        give(d).start()
        return carry

    lax.fori_loop(1, n, serve, 0)
    for p in range(3):
        tiles_ref[me, p] = choose(me, p)

    def finish(d, carry):
        ask(d).wait_send()
        give(d).wait_send()
        given_by(d).wait_recv()
        return carry

    lax.fori_loop(1, n, finish, 0)


def fetch(wanted, planes, n):
    pieces = planes.shape[2] // BLK
    tiles_dev = planes.shape[1]
    vmem = pl.BlockSpec(memory_space=pltpu.VMEM)
    return pl.pallas_call(
        functools.partial(fetch_kernel, n),
        out_shape=(
            jax.ShapeDtypeStruct((n, 3, pieces, BLK), BF16),
            jax.ShapeDtypeStruct((n, 8, BLK), F32),
        ),
        in_specs=[pl.BlockSpec(memory_space=pltpu.SMEM), vmem],
        out_specs=(vmem, vmem),
        scratch_shapes=[
            pltpu.VMEM((n, 8, BLK), F32),
            pltpu.VMEM((3, tiles_dev, pieces, BLK), F32),
            pltpu.VMEM((3, tiles_dev, pieces, BLK), BF16),
            pltpu.VMEM((n, 3, pieces, BLK), BF16),
        ]
        + [pltpu.SemaphoreType.DMA((n,))] * 4,
        compiler_params=pltpu.CompilerParams(
            collective_id=0, has_side_effects=True, vmem_limit_bytes=24 * 1024 * 1024
        ),
        name="fetch_tiles",
    )(wanted, planes)


def give_back_kernel(n, sums_ref, asked_ref, out_ref, outgoing, landed, total, send_sem, recv_sem):
    me = lax.axis_index("tile")
    tiles_dev = out_ref.shape[1]
    pieces = out_ref.shape[2] // BLK

    def fill(o, carry):
        outgoing[o] = sums_ref[o].astype(BF16)
        return carry

    lax.fori_loop(0, n, fill, 0)
    enter(n)

    def give(d):
        to = lax.rem(me + d, n)
        return pltpu.make_async_remote_copy(
            src_ref=outgoing.at[to], dst_ref=landed.at[me], send_sem=send_sem.at[d], recv_sem=recv_sem.at[d],
            device_id=peer(d, n), device_id_type=pl.DeviceIdType.MESH,
        )

    def given_by(d):
        source = lax.rem(me - d + n, n)
        return pltpu.make_async_remote_copy(
            src_ref=outgoing.at[source], dst_ref=landed.at[source], send_sem=send_sem.at[d],
            recv_sem=recv_sem.at[d], device_id=peer(d, n), device_id_type=pl.DeviceIdType.MESH,
        )

    def start(d, carry):
        give(d).start()
        return carry

    lax.fori_loop(1, n, start, 0)

    for p in range(3):
        mine = sums_ref[me, p]
        want = jnp.broadcast_to(asked_ref[me, p : p + 1, :], (pieces, BLK))
        for k in range(tiles_dev):
            total[p, k] = jnp.where(want == k, mine, 0.0)

    def add(d, carry):
        given_by(d).wait_recv()
        source = lax.rem(me - d + n, n)
        for p in range(3):
            came = landed[source, p].astype(F32)
            want = jnp.broadcast_to(asked_ref[source, p : p + 1, :], (pieces, BLK))
            for k in range(tiles_dev):
                total[p, k] += jnp.where(want == k, came, 0.0)
        return carry

    lax.fori_loop(1, n, add, 0)
    for p in range(3):
        for i in range(pieces):
            out_ref[p, :, i * BLK : (i + 1) * BLK] = total[p, :, i, :]

    def finish(d, carry):
        give(d).wait_send()
        return carry

    lax.fori_loop(1, n, finish, 0)


def give_back(sums, asked, tiles_dev, n):
    pieces = sums.shape[2]
    vmem = pl.BlockSpec(memory_space=pltpu.VMEM)
    return pl.pallas_call(
        functools.partial(give_back_kernel, n),
        out_shape=jax.ShapeDtypeStruct((3, tiles_dev, pieces * BLK), F32),
        in_specs=[vmem, vmem],
        out_specs=vmem,
        scratch_shapes=[
            pltpu.VMEM((n, 3, pieces, BLK), BF16),
            pltpu.VMEM((n, 3, pieces, BLK), BF16),
            pltpu.VMEM((3, tiles_dev, pieces, BLK), F32),
            pltpu.SemaphoreType.DMA((n,)),
            pltpu.SemaphoreType.DMA((n,)),
        ],
        compiler_params=pltpu.CompilerParams(
            collective_id=1, has_side_effects=True, vmem_limit_bytes=24 * 1024 * 1024
        ),
        name="give_back",
    )(sums, asked)


def shards(planes, decoder_in, decoder_out, corner, fraction, block_slot, wanted, ray_id, ray_grad):
    owners = lax.axis_size("tile")
    tiles, asked = fetch(wanted.reshape(-1), planes, owners)
    slot_sums = compute(block_slot, tiles, decoder_in, decoder_out, ray_grad[0], corner, fraction, ray_id)
    return give_back(slot_sums, asked, planes.shape[1], owners)


def solution(mesh):
    placed = (
        P(None, ("parts", "tile"), None),
        P(),
        P(),
        P(None, ("parts", "tile")),
        P(None, None, ("parts", "tile")),
        P(None, ("parts", "tile")),
        P(("parts", "tile"), None, None, None),
        P(("parts", "tile"), None),
        P(("parts", "tile"), None, None),
    )
    return jax.shard_map(
        shards,
        mesh=mesh,
        in_specs=placed,
        out_specs=P(None, ("parts", "tile"), None),
        check_vma=False,
    )
```

```python
import functools

import jax
import jax.numpy as jnp
from jax import lax
from jax.experimental import pallas as pl
from jax.experimental.pallas import tpu as pltpu
from jax.sharding import PartitionSpec as P

OUTS = 4
TS = 8
BLK = 128
CHUNK = 8192
GROUP = 32

F32 = jnp.float32
BF16 = jnp.bfloat16


def cell_weights(corner_row, across, downward):
    row = (corner_row * 37) >> 8
    col = corner_row - row * (TS - 1)
    sub = lax.broadcasted_iota(jnp.int32, (TS, BLK), 0)
    col8 = jnp.broadcast_to(col, (TS, BLK))
    side = jnp.where(sub == col8, 1.0 - across, jnp.where(sub == col8 + 1, across, 0.0))
    upper = side * (1.0 - downward)
    lower = side * downward
    upper = jnp.concatenate([upper, upper], axis=0).astype(BF16)
    lower = jnp.concatenate([lower, lower], axis=0).astype(BF16)
    row8 = jnp.broadcast_to(row, (TS, BLK)).astype(F32)
    rows = jnp.concatenate([row8, row8 - 1.0], axis=0).astype(BF16)
    zero = jnp.zeros((2 * TS, BLK), BF16)
    pairs = []
    for first in range(0, TS, 2):
        here = rows == jnp.asarray(first, BF16)
        above = rows == jnp.asarray(first - 1, BF16)
        pairs.append(jnp.where(here, upper, jnp.where(above, lower, zero)))
    return jnp.concatenate(pairs, axis=0)


def dot(a, b):
    return jnp.dot(a, b, preferred_element_type=F32)


def dot_t(a, b):
    return lax.dot_general(a, b, (((1,), (1,)), ((), ())), preferred_element_type=F32)


def compute_kernel(
    slots_ref, tiles_ref, win_ref, wout_ref, grad_ref, corner_ref, fraction_ref, ray_ref, acc_ref,
    win_t, win, wout, table, *sums
):
    step = pl.program_id(0)
    halves = table.shape[0]
    channels = win_ref.shape[0]
    half_c = channels // 2

    @pl.when(step == 0)
    def _():
        for one in sums:
            one[...] = jnp.zeros_like(one)
        by_parity = jnp.concatenate(
            [win_ref[pl.ds(0, half_c, stride=2), :], win_ref[pl.ds(1, half_c, stride=2), :]], axis=0
        )
        win[...] = by_parity.astype(BF16)
        win_t[...] = (by_parity.T * 0.5).astype(BF16)
        out_at = lax.broadcasted_iota(jnp.int32, (OUTS, 2 * OUTS * halves), 0)
        copy_at = lax.broadcasted_iota(jnp.int32, (OUTS, 2 * OUTS * halves), 1) % OUTS
        repeat = jnp.where(out_at == copy_at, 0.5, 0.0).astype(BF16)
        wout[...] = dot(wout_ref[...].astype(BF16), repeat).astype(BF16)
        for h in range(halves):
            for k in range(2):
                first = (2 * h + k) * BLK
                table[h, k * OUTS : (k + 1) * OUTS, :] = grad_ref[0, :, first : first + BLK]

    blocks = CHUNK // BLK
    rows = table.shape[1]

    def body(at, carry):
        slots = [
            [slots_ref[p, step * blocks + at * GROUP + b] for p in range(3)] for b in range(GROUP)
        ]
        lanes = [
            pl.ds(pl.multiple_of((at * GROUP + b) * BLK, BLK), BLK) for b in range(GROUP)
        ]
        wide, grads_out = [], []
        feats = [[None] * 3 for b in range(GROUP)]
        for b in range(GROUP):
            wides = []
            for p in range(3):
                m = cell_weights(
                    corner_ref[p : p + 1, lanes[b]],
                    fraction_ref[p, 0:1, lanes[b]],
                    fraction_ref[p, 1:2, lanes[b]],
                )
                z = jnp.zeros_like(m)
                w = jnp.concatenate(
                    [jnp.concatenate([m, z], axis=1), jnp.concatenate([z, m], axis=1)], axis=0
                )
                wides.append(m)
                f = dot(tiles_ref[slots[b][p], p], w)
                feats[b][p] = jnp.concatenate([f[:, :BLK], f[:, BLK:]], axis=0)
            wide.append(wides)
            ray = ray_ref[0:1, lanes[b]]
            picks = []
            idx = jnp.broadcast_to(ray & (BLK - 1), (rows, BLK))
            part = jnp.broadcast_to(ray >> 7, (rows, BLK))
            sub = lax.broadcasted_iota(jnp.int32, (rows, BLK), 0) // OUTS
            for h in range(halves):
                got = jnp.take_along_axis(table[h], idx, axis=1)
                picks.append(jnp.where(part == sub + 2 * h, got, 0.0))
            grads_out.append(jnp.concatenate(picks, axis=0))
        f = [jnp.concatenate([feats[b][p] for b in range(GROUP)], axis=1) for p in range(3)]
        others = [f[1] * f[2], f[0] * f[2], f[0] * f[1]]
        product = (others[2] * f[2]).astype(BF16)
        grads_out = jnp.concatenate(grads_out, axis=1).astype(BF16)
        half_pre = dot(win_t[...], product)
        hidden = dot(wout[...], grads_out)
        t = jnp.tanh(half_pre)
        pre_grad = hidden * ((1.0 + t) * (1.0 + half_pre * (1.0 - t)))
        prod_grad = dot(win[...], pre_grad.astype(BF16))
        for p in range(3):
            fg = (prod_grad * others[p]).astype(BF16)
            for b in range(GROUP):
                piece = fg[:, b * BLK : (b + 1) * BLK]
                sums[p][slots[b][p]] += dot_t(piece, wide[b][p])
        return carry

    lax.fori_loop(0, blocks // GROUP, body, 0)

    @pl.when(step == pl.num_programs(0) - 1)
    def _():
        for p in range(3):
            def put(k, carry):
                one = sums[p][k]
                acc_ref[k, p] = jnp.concatenate([one[:half_c], one[half_c:]], axis=1).astype(acc_ref.dtype)
                return carry

            lax.fori_loop(0, acc_ref.shape[0], put, 0)


def compute(slots, tiles, decoder_in, decoder_out, ray_grad, corner, fraction, ray_id):
    channels, hid = decoder_in.shape
    samples = corner.shape[1]
    halves = ray_grad.shape[2] // (2 * BLK)
    steps = samples // CHUNK
    vmem = pl.BlockSpec(memory_space=pltpu.VMEM)
    grid_spec = pltpu.PrefetchScalarGridSpec(
        num_scalar_prefetch=1,
        grid=(steps,),
        in_specs=[
            vmem,
            vmem,
            vmem,
            vmem,
            pl.BlockSpec((3, CHUNK), lambda i, s: (0, i)),
            pl.BlockSpec((3, 2, CHUNK), lambda i, s: (0, 0, i)),
            pl.BlockSpec((1, CHUNK), lambda i, s: (0, i)),
        ],
        out_specs=pl.BlockSpec(tiles.shape, lambda i, s: (0, 0, 0, 0)),
        scratch_shapes=[
            pltpu.VMEM((hid, channels), BF16),
            pltpu.VMEM((channels, hid), BF16),
            pltpu.VMEM((hid, 2 * OUTS * halves), BF16),
            pltpu.VMEM((halves, 2 * OUTS, BLK), F32),
        ]
        + [pltpu.VMEM((tiles.shape[0],) + (channels, TS * TS), F32)] * 3,
    )
    return pl.pallas_call(
        compute_kernel,
        grid_spec=grid_spec,
        out_shape=jax.ShapeDtypeStruct(tiles.shape, BF16),
        compiler_params=pltpu.CompilerParams(vmem_limit_bytes=60 * 1024 * 1024),
        name="field_grad",
    )(slots, tiles, decoder_in, decoder_out, ray_grad, corner, fraction, ray_id)


def peer(d, n):
    return {"tile": lax.rem(lax.axis_index("tile") + d, n)}


def enter(n):
    barrier = pltpu.get_barrier_semaphore()

    def tell(d, carry):
        pl.semaphore_signal(barrier, inc=1, device_id=peer(d, n), device_id_type=pl.DeviceIdType.MESH)
        return carry

    lax.fori_loop(1, n, tell, 0)
    pl.semaphore_wait(barrier, n - 1)


def fetch_kernel(
    n, wanted_ref, planes_ref, tiles_ref, asked_ref,
    asking, spread, own, outgoing, ask_send, ask_recv, tile_send, tile_recv,
):
    me = lax.axis_index("tile")
    tiles_dev = planes_ref.shape[1]
    pieces = planes_ref.shape[2] // BLK

    def fill(o, carry):
        for p in range(3):
            asking[o, p : p + 1, :] = jnp.full((1, BLK), wanted_ref[p * n + o], jnp.int32).astype(F32)
        return carry

    asking[...] = jnp.zeros_like(asking)
    lax.fori_loop(0, n, fill, 0)
    enter(n)

    def ask(d):
        to = lax.rem(me + d, n)
        return pltpu.make_async_remote_copy(
            src_ref=asking.at[to], dst_ref=asked_ref.at[me], send_sem=ask_send.at[d], recv_sem=ask_recv.at[d],
            device_id=peer(d, n), device_id_type=pl.DeviceIdType.MESH,
        )

    def asked_by(d):
        source = lax.rem(me - d + n, n)
        return pltpu.make_async_remote_copy(
            src_ref=asking.at[source], dst_ref=asked_ref.at[source], send_sem=ask_send.at[d],
            recv_sem=ask_recv.at[d], device_id=peer(d, n), device_id_type=pl.DeviceIdType.MESH,
        )

    def give(d):
        to = lax.rem(me - d + n, n)
        return pltpu.make_async_remote_copy(
            src_ref=outgoing.at[to], dst_ref=tiles_ref.at[me], send_sem=tile_send.at[d],
            recv_sem=tile_recv.at[d], device_id=peer(n - d, n), device_id_type=pl.DeviceIdType.MESH,
        )

    def given_by(d):
        source = lax.rem(me + d, n)
        return pltpu.make_async_remote_copy(
            src_ref=outgoing.at[source], dst_ref=tiles_ref.at[source], send_sem=tile_send.at[d],
            recv_sem=tile_recv.at[d], device_id=peer(n - d, n), device_id_type=pl.DeviceIdType.MESH,
        )

    def start_ask(d, carry):
        ask(d).start()
        return carry

    lax.fori_loop(1, n, start_ask, 0)
    asked_ref[me] = asking[me]
    for p in range(3):
        wide = planes_ref[p].astype(F32)
        for i in range(pieces):
            spread[p, :, i, :] = wide[:, i * BLK : (i + 1) * BLK]
    own[...] = spread[...].astype(BF16)

    def choose(source, p):
        want = jnp.broadcast_to(asked_ref[source, p : p + 1, :], (pieces, BLK)).astype(BF16)
        got = jnp.zeros((pieces, BLK), BF16)
        for k in range(tiles_dev):
            got = jnp.where(want == jnp.asarray(k, BF16), own[p, k], got)
        return got

    def serve(d, carry):
        asked_by(d).wait_recv()
        to = lax.rem(me - d + n, n)
        for p in range(3):
            outgoing[to, p] = choose(to, p)
        give(d).start()
        return carry

    lax.fori_loop(1, n, serve, 0)
    for p in range(3):
        tiles_ref[me, p] = choose(me, p)

    def finish(d, carry):
        ask(d).wait_send()
        give(d).wait_send()
        given_by(d).wait_recv()
        return carry

    lax.fori_loop(1, n, finish, 0)


def fetch(wanted, planes, n):
    pieces = planes.shape[2] // BLK
    tiles_dev = planes.shape[1]
    vmem = pl.BlockSpec(memory_space=pltpu.VMEM)
    return pl.pallas_call(
        functools.partial(fetch_kernel, n),
        out_shape=(
            jax.ShapeDtypeStruct((n, 3, pieces, BLK), BF16),
            jax.ShapeDtypeStruct((n, 8, BLK), F32),
        ),
        in_specs=[pl.BlockSpec(memory_space=pltpu.SMEM), vmem],
        out_specs=(vmem, vmem),
        scratch_shapes=[
            pltpu.VMEM((n, 8, BLK), F32),
            pltpu.VMEM((3, tiles_dev, pieces, BLK), F32),
            pltpu.VMEM((3, tiles_dev, pieces, BLK), BF16),
            pltpu.VMEM((n, 3, pieces, BLK), BF16),
        ]
        + [pltpu.SemaphoreType.DMA((n,))] * 4,
        compiler_params=pltpu.CompilerParams(
            collective_id=0, has_side_effects=True, vmem_limit_bytes=24 * 1024 * 1024
        ),
        name="fetch_tiles",
    )(wanted, planes)


def give_back_kernel(n, sums_ref, asked_ref, out_ref, landed, total, send_sem, recv_sem):
    me = lax.axis_index("tile")
    tiles_dev = out_ref.shape[1]
    pieces = out_ref.shape[2] // BLK

    enter(n)

    def give(d):
        to = lax.rem(me + d, n)
        return pltpu.make_async_remote_copy(
            src_ref=sums_ref.at[to], dst_ref=landed.at[me], send_sem=send_sem.at[d], recv_sem=recv_sem.at[d],
            device_id=peer(d, n), device_id_type=pl.DeviceIdType.MESH,
        )

    def given_by(d):
        source = lax.rem(me - d + n, n)
        return pltpu.make_async_remote_copy(
            src_ref=sums_ref.at[source], dst_ref=landed.at[source], send_sem=send_sem.at[d],
            recv_sem=recv_sem.at[d], device_id=peer(d, n), device_id_type=pl.DeviceIdType.MESH,
        )

    def start(d, carry):
        give(d).start()
        return carry

    lax.fori_loop(1, n, start, 0)

    for p in range(3):
        mine = sums_ref[me, p].astype(F32)
        want = jnp.broadcast_to(asked_ref[me, p : p + 1, :], (pieces, BLK))
        for k in range(tiles_dev):
            total[p, k] = jnp.where(want == k, mine, 0.0)

    def add(d, carry):
        given_by(d).wait_recv()
        source = lax.rem(me - d + n, n)
        for p in range(3):
            came = landed[source, p].astype(F32)
            want = jnp.broadcast_to(asked_ref[source, p : p + 1, :], (pieces, BLK))
            for k in range(tiles_dev):
                total[p, k] += jnp.where(want == k, came, 0.0)
        return carry

    lax.fori_loop(1, n, add, 0)
    for p in range(3):
        for i in range(pieces):
            out_ref[p, :, i * BLK : (i + 1) * BLK] = total[p, :, i, :]

    def finish(d, carry):
        give(d).wait_send()
        return carry

    lax.fori_loop(1, n, finish, 0)


def give_back(sums, asked, tiles_dev, n):
    pieces = sums.shape[2]
    vmem = pl.BlockSpec(memory_space=pltpu.VMEM)
    return pl.pallas_call(
        functools.partial(give_back_kernel, n),
        out_shape=jax.ShapeDtypeStruct((3, tiles_dev, pieces * BLK), F32),
        in_specs=[vmem, vmem],
        out_specs=vmem,
        scratch_shapes=[
            pltpu.VMEM((n, 3, pieces, BLK), BF16),
            pltpu.VMEM((3, tiles_dev, pieces, BLK), F32),
            pltpu.SemaphoreType.DMA((n,)),
            pltpu.SemaphoreType.DMA((n,)),
        ],
        compiler_params=pltpu.CompilerParams(
            collective_id=1, has_side_effects=True, vmem_limit_bytes=24 * 1024 * 1024
        ),
        name="give_back",
    )(sums, asked)


def shards(planes, decoder_in, decoder_out, corner, fraction, block_slot, wanted, ray_id, ray_grad):
    owners = lax.axis_size("tile")
    tiles, asked = fetch(wanted.reshape(-1), planes, owners)
    slot_sums = compute(block_slot, tiles, decoder_in, decoder_out, ray_grad, corner, fraction, ray_id)
    return give_back(slot_sums, asked, planes.shape[1], owners)


def solution(mesh):
    placed = (
        P(None, ("parts", "tile"), None),
        P(),
        P(),
        P(None, ("parts", "tile")),
        P(None, None, ("parts", "tile")),
        P(None, ("parts", "tile")),
        P(("parts", "tile"), None, None, None),
        P(("parts", "tile"), None),
        P(("parts", "tile"), None, None),
    )
    return jax.shard_map(
        shards,
        mesh=mesh,
        in_specs=placed,
        out_specs=P(None, ("parts", "tile"), None),
        check_vma=False,
    )
```

```python
import functools

import jax
import jax.numpy as jnp
from jax import lax
from jax.experimental import pallas as pl
from jax.experimental.pallas import tpu as pltpu
from jax.sharding import PartitionSpec as P

OUTS = 4
TS = 8
BLK = 128
CHUNK = 16384
GROUP = 64

F32 = jnp.float32
BF16 = jnp.bfloat16


def cell_weights(corner_row, across, downward):
    row = (corner_row * 37) >> 8
    col = corner_row - row * (TS - 1)
    sub = lax.broadcasted_iota(jnp.int32, (TS, BLK), 0)
    col8 = jnp.broadcast_to(col, (TS, BLK))
    side = jnp.where(sub == col8, 1.0 - across, jnp.where(sub == col8 + 1, across, 0.0))
    upper = side * (1.0 - downward)
    lower = side * downward
    upper = jnp.concatenate([upper, upper], axis=0).astype(BF16)
    lower = jnp.concatenate([lower, lower], axis=0).astype(BF16)
    row8 = jnp.broadcast_to(row, (TS, BLK)).astype(F32)
    rows = jnp.concatenate([row8, row8 - 1.0], axis=0).astype(BF16)
    zero = jnp.zeros((2 * TS, BLK), BF16)
    pairs = []
    for first in range(0, TS, 2):
        here = rows == jnp.asarray(first, BF16)
        above = rows == jnp.asarray(first - 1, BF16)
        pairs.append(jnp.where(here, upper, jnp.where(above, lower, zero)))
    return jnp.concatenate(pairs, axis=0)


def dot(a, b):
    return jnp.dot(a, b, preferred_element_type=F32)


def dot_t(a, b):
    return lax.dot_general(a, b, (((1,), (1,)), ((), ())), preferred_element_type=F32)


def compute_kernel(
    slots_ref, tiles_ref, win_ref, wout_ref, grad_ref, corner_ref, fraction_ref, ray_ref, acc_ref,
    win_t, win, wout, table, *sums
):
    step = pl.program_id(0)
    halves = table.shape[0]
    channels = win_ref.shape[0]
    half_c = channels // 2

    @pl.when(step == 0)
    def _():
        for one in sums:
            one[...] = jnp.zeros_like(one)
        by_parity = jnp.concatenate(
            [win_ref[pl.ds(0, half_c, stride=2), :], win_ref[pl.ds(1, half_c, stride=2), :]], axis=0
        )
        win[...] = by_parity.astype(BF16)
        win_t[...] = (by_parity.T * 0.5).astype(BF16)
        out_at = lax.broadcasted_iota(jnp.int32, (OUTS, 2 * OUTS * halves), 0)
        copy_at = lax.broadcasted_iota(jnp.int32, (OUTS, 2 * OUTS * halves), 1) % OUTS
        repeat = jnp.where(out_at == copy_at, 0.5, 0.0).astype(BF16)
        wout[...] = lax.dot_general(
            wout_ref[...].astype(BF16), repeat, (((0,), (0,)), ((), ())), preferred_element_type=F32
        ).astype(BF16)
        for h in range(halves):
            for k in range(2):
                first = (2 * h + k) * BLK
                table[h, k * OUTS : (k + 1) * OUTS, :] = grad_ref[0, :, first : first + BLK]

    blocks = CHUNK // BLK
    rows = table.shape[1]

    def body(at, carry):
        slots = [
            [slots_ref[p, step * blocks + at * GROUP + b] for p in range(3)] for b in range(GROUP)
        ]
        lanes = [
            pl.ds(pl.multiple_of((at * GROUP + b) * BLK, BLK), BLK) for b in range(GROUP)
        ]
        wide, grads_out = [], []
        feats = [[None] * 3 for b in range(GROUP)]
        for b in range(GROUP):
            wides = []
            for p in range(3):
                m = cell_weights(
                    corner_ref[p : p + 1, lanes[b]],
                    fraction_ref[p, 0:1, lanes[b]],
                    fraction_ref[p, 1:2, lanes[b]],
                )
                z = jnp.zeros_like(m)
                w = jnp.concatenate(
                    [jnp.concatenate([m, z], axis=1), jnp.concatenate([z, m], axis=1)], axis=0
                )
                wides.append(m)
                f = dot(tiles_ref[slots[b][p], p], w)
                feats[b][p] = jnp.concatenate([f[:, :BLK], f[:, BLK:]], axis=0)
            wide.append(wides)
            ray = ray_ref[0:1, lanes[b]]
            picks = []
            idx = jnp.broadcast_to(ray & (BLK - 1), (rows, BLK))
            part = jnp.broadcast_to(ray >> 7, (rows, BLK))
            sub = lax.broadcasted_iota(jnp.int32, (rows, BLK), 0) // OUTS
            for h in range(halves):
                got = jnp.take_along_axis(table[h], idx, axis=1)
                picks.append(jnp.where(part == sub + 2 * h, got, 0.0))
            grads_out.append(jnp.concatenate(picks, axis=0))
        f = [jnp.concatenate([feats[b][p] for b in range(GROUP)], axis=1) for p in range(3)]
        others = [f[1] * f[2], f[0] * f[2], f[0] * f[1]]
        product = (others[2] * f[2]).astype(BF16)
        grads_out = jnp.concatenate(grads_out, axis=1).astype(BF16)
        half_pre = dot(win_t[...], product)
        hidden = dot(wout[...], grads_out)
        t = jnp.tanh(half_pre)
        pre_grad = hidden * ((1.0 + t) * (1.0 + half_pre * (1.0 - t)))
        prod_grad = dot(win[...], pre_grad.astype(BF16))
        for p in range(3):
            fg = (prod_grad * others[p]).astype(BF16)
            for b in range(GROUP):
                piece = fg[:, b * BLK : (b + 1) * BLK]
                sums[p][slots[b][p]] += dot_t(piece, wide[b][p])
        return carry

    lax.fori_loop(0, blocks // GROUP, body, 0)

    @pl.when(step == pl.num_programs(0) - 1)
    def _():
        for p in range(3):
            def put(k, carry):
                one = sums[p][k]
                acc_ref[k, p] = jnp.concatenate([one[:half_c], one[half_c:]], axis=1).astype(acc_ref.dtype)
                return carry

            lax.fori_loop(0, acc_ref.shape[0], put, 0)


def compute(slots, tiles, decoder_in, decoder_out, ray_grad, corner, fraction, ray_id):
    channels, hid = decoder_in.shape
    samples = corner.shape[1]
    halves = ray_grad.shape[2] // (2 * BLK)
    steps = samples // CHUNK
    vmem = pl.BlockSpec(memory_space=pltpu.VMEM)
    grid_spec = pltpu.PrefetchScalarGridSpec(
        num_scalar_prefetch=1,
        grid=(steps,),
        in_specs=[
            vmem,
            vmem,
            vmem,
            vmem,
            pl.BlockSpec((3, CHUNK), lambda i, s: (0, i)),
            pl.BlockSpec((3, 2, CHUNK), lambda i, s: (0, 0, i)),
            pl.BlockSpec((1, CHUNK), lambda i, s: (0, i)),
        ],
        out_specs=pl.BlockSpec(tiles.shape, lambda i, s: (0, 0, 0, 0)),
        scratch_shapes=[
            pltpu.VMEM((hid, channels), BF16),
            pltpu.VMEM((channels, hid), BF16),
            pltpu.VMEM((hid, 2 * OUTS * halves), BF16),
            pltpu.VMEM((halves, 2 * OUTS, BLK), F32),
        ]
        + [pltpu.VMEM((tiles.shape[0],) + (channels, TS * TS), F32)] * 3,
    )
    return pl.pallas_call(
        compute_kernel,
        grid_spec=grid_spec,
        out_shape=jax.ShapeDtypeStruct(tiles.shape, BF16),
        compiler_params=pltpu.CompilerParams(vmem_limit_bytes=60 * 1024 * 1024),
        name="field_grad",
    )(slots, tiles, decoder_in, decoder_out.T, ray_grad, corner, fraction, ray_id)


def peer(d, n):
    return {"tile": lax.rem(lax.axis_index("tile") + d, n)}


def enter(n):
    barrier = pltpu.get_barrier_semaphore()

    def tell(d, carry):
        pl.semaphore_signal(barrier, inc=1, device_id=peer(d, n), device_id_type=pl.DeviceIdType.MESH)
        return carry

    lax.fori_loop(1, n, tell, 0)
    pl.semaphore_wait(barrier, n - 1)


def fetch_kernel(
    n, wanted_ref, planes_ref, tiles_ref, asked_ref,
    asking, spread, own, outgoing, ask_send, ask_recv, tile_send, tile_recv,
):
    me = lax.axis_index("tile")
    tiles_dev = planes_ref.shape[1]
    pieces = planes_ref.shape[2] // BLK

    def fill(o, carry):
        for p in range(3):
            asking[o, p : p + 1, :] = jnp.full((1, BLK), wanted_ref[p * n + o], jnp.int32).astype(F32)
        return carry

    asking[...] = jnp.zeros_like(asking)
    lax.fori_loop(0, n, fill, 0)
    enter(n)

    def ask(d):
        to = lax.rem(me + d, n)
        return pltpu.make_async_remote_copy(
            src_ref=asking.at[to], dst_ref=asked_ref.at[me], send_sem=ask_send.at[d], recv_sem=ask_recv.at[d],
            device_id=peer(d, n), device_id_type=pl.DeviceIdType.MESH,
        )

    def asked_by(d):
        source = lax.rem(me - d + n, n)
        return pltpu.make_async_remote_copy(
            src_ref=asking.at[source], dst_ref=asked_ref.at[source], send_sem=ask_send.at[d],
            recv_sem=ask_recv.at[d], device_id=peer(d, n), device_id_type=pl.DeviceIdType.MESH,
        )

    def give(d):
        to = lax.rem(me - d + n, n)
        return pltpu.make_async_remote_copy(
            src_ref=outgoing.at[to], dst_ref=tiles_ref.at[me], send_sem=tile_send.at[d],
            recv_sem=tile_recv.at[d], device_id=peer(n - d, n), device_id_type=pl.DeviceIdType.MESH,
        )

    def given_by(d):
        source = lax.rem(me + d, n)
        return pltpu.make_async_remote_copy(
            src_ref=outgoing.at[source], dst_ref=tiles_ref.at[source], send_sem=tile_send.at[d],
            recv_sem=tile_recv.at[d], device_id=peer(n - d, n), device_id_type=pl.DeviceIdType.MESH,
        )

    def start_ask(d, carry):
        ask(d).start()
        return carry

    lax.fori_loop(1, n, start_ask, 0)
    asked_ref[me] = asking[me]
    for p in range(3):
        wide = planes_ref[p].astype(F32)
        for i in range(pieces):
            spread[p, :, i, :] = wide[:, i * BLK : (i + 1) * BLK]
    own[...] = spread[...].astype(BF16)

    def choose(source, p):
        want = jnp.broadcast_to(asked_ref[source, p : p + 1, :], (pieces, BLK)).astype(BF16)
        got = jnp.zeros((pieces, BLK), BF16)
        for k in range(tiles_dev):
            got = jnp.where(want == jnp.asarray(k, BF16), own[p, k], got)
        return got

    def serve(d, carry):
        asked_by(d).wait_recv()
        to = lax.rem(me - d + n, n)
        for p in range(3):
            outgoing[to, p] = choose(to, p)
        give(d).start()
        return carry

    lax.fori_loop(1, n, serve, 0)
    for p in range(3):
        tiles_ref[me, p] = choose(me, p)

    def finish(d, carry):
        ask(d).wait_send()
        give(d).wait_send()
        given_by(d).wait_recv()
        return carry

    lax.fori_loop(1, n, finish, 0)


def fetch(wanted, planes, n):
    pieces = planes.shape[2] // BLK
    tiles_dev = planes.shape[1]
    vmem = pl.BlockSpec(memory_space=pltpu.VMEM)
    return pl.pallas_call(
        functools.partial(fetch_kernel, n),
        out_shape=(
            jax.ShapeDtypeStruct((n, 3, pieces, BLK), BF16),
            jax.ShapeDtypeStruct((n, 8, BLK), F32),
        ),
        in_specs=[pl.BlockSpec(memory_space=pltpu.SMEM), vmem],
        out_specs=(vmem, vmem),
        scratch_shapes=[
            pltpu.VMEM((n, 8, BLK), F32),
            pltpu.VMEM((3, tiles_dev, pieces, BLK), F32),
            pltpu.VMEM((3, tiles_dev, pieces, BLK), BF16),
            pltpu.VMEM((n, 3, pieces, BLK), BF16),
        ]
        + [pltpu.SemaphoreType.DMA((n,))] * 4,
        compiler_params=pltpu.CompilerParams(
            collective_id=0, has_side_effects=True, vmem_limit_bytes=24 * 1024 * 1024
        ),
        name="fetch_tiles",
    )(wanted, planes)


def give_back_kernel(n, sums_ref, asked_ref, out_ref, landed, total, send_sem, recv_sem):
    me = lax.axis_index("tile")
    tiles_dev = out_ref.shape[1]
    pieces = out_ref.shape[2] // BLK

    enter(n)

    def give(d):
        to = lax.rem(me + d, n)
        return pltpu.make_async_remote_copy(
            src_ref=sums_ref.at[to], dst_ref=landed.at[me], send_sem=send_sem.at[d], recv_sem=recv_sem.at[d],
            device_id=peer(d, n), device_id_type=pl.DeviceIdType.MESH,
        )

    def given_by(d):
        source = lax.rem(me - d + n, n)
        return pltpu.make_async_remote_copy(
            src_ref=sums_ref.at[source], dst_ref=landed.at[source], send_sem=send_sem.at[d],
            recv_sem=recv_sem.at[d], device_id=peer(d, n), device_id_type=pl.DeviceIdType.MESH,
        )

    def start(d, carry):
        give(d).start()
        return carry

    lax.fori_loop(1, n, start, 0)

    for p in range(3):
        mine = sums_ref[me, p].astype(F32)
        want = jnp.broadcast_to(asked_ref[me, p : p + 1, :], (pieces, BLK))
        for k in range(tiles_dev):
            total[p, k] = jnp.where(want == k, mine, 0.0)

    def add(d, carry):
        given_by(d).wait_recv()
        source = lax.rem(me - d + n, n)
        for p in range(3):
            came = landed[source, p].astype(F32)
            want = jnp.broadcast_to(asked_ref[source, p : p + 1, :], (pieces, BLK))
            for k in range(tiles_dev):
                total[p, k] += jnp.where(want == k, came, 0.0)
        return carry

    lax.fori_loop(1, n, add, 0)
    for p in range(3):
        for i in range(pieces):
            out_ref[p, :, i * BLK : (i + 1) * BLK] = total[p, :, i, :]

    def finish(d, carry):
        give(d).wait_send()
        return carry

    lax.fori_loop(1, n, finish, 0)


def give_back(sums, asked, tiles_dev, n):
    pieces = sums.shape[2]
    vmem = pl.BlockSpec(memory_space=pltpu.VMEM)
    return pl.pallas_call(
        functools.partial(give_back_kernel, n),
        out_shape=jax.ShapeDtypeStruct((3, tiles_dev, pieces * BLK), F32),
        in_specs=[vmem, vmem],
        out_specs=vmem,
        scratch_shapes=[
            pltpu.VMEM((n, 3, pieces, BLK), BF16),
            pltpu.VMEM((3, tiles_dev, pieces, BLK), F32),
            pltpu.SemaphoreType.DMA((n,)),
            pltpu.SemaphoreType.DMA((n,)),
        ],
        compiler_params=pltpu.CompilerParams(
            collective_id=1, has_side_effects=True, vmem_limit_bytes=24 * 1024 * 1024
        ),
        name="give_back",
    )(sums, asked)


def shards(planes, decoder_in, decoder_out, corner, fraction, block_slot, wanted, ray_id, ray_grad):
    owners = lax.axis_size("tile")
    tiles, asked = fetch(wanted.reshape(-1), planes, owners)
    slot_sums = compute(block_slot, tiles, decoder_in, decoder_out, ray_grad, corner, fraction, ray_id)
    return give_back(slot_sums, asked, planes.shape[1], owners)


def solution(mesh):
    placed = (
        P(None, ("parts", "tile"), None),
        P(),
        P(),
        P(None, ("parts", "tile")),
        P(None, None, ("parts", "tile")),
        P(None, ("parts", "tile")),
        P(("parts", "tile"), None, None, None),
        P(("parts", "tile"), None),
        P(("parts", "tile"), None, None),
    )
    return jax.shard_map(
        shards,
        mesh=mesh,
        in_specs=placed,
        out_specs=P(None, ("parts", "tile"), None),
        check_vma=False,
    )
```
